32 devices in a mesh: groups: 2 (over x), pool: 16 (over z, y, core).
Axes of the slice: x: 2, y: 2, z: 4, core: 2. Of those that a mesh axis runs over, the one named last changes fastest.
Arguments:
- hidden: bfloat16 [2, 32, 8192], P(None, 'groups', 'pool'), parts along dimension 1, may hold values from -6 to 6
- norm_gain_vector: float32 [8192], replicated, may hold values from 0.1 to 1.9
- query_key_value_weight: bfloat16 [8192, 10240], P('pool'), may hold values from -0.0625 to 0.0625
- output_weight: bfloat16 [8192, 8192], P(None, 'pool'), may hold values from -0.0625 to 0.0625
- key_value_cache: bfloat16 [32, 256, 2048], P(('groups', 'pool')), parts along dimension 0, may hold values from -60 to 60
- cache_valid_length: int32 [32], P(('groups', 'pool')), parts along dimension 0, may hold values from 1 to 256, as said below
- request_adapter_index: int32 [2, 32, 1], P(None, 'groups'), parts along dimension 1, may hold values from 0 to 15
- adapter_slot_place: int32 [32], P('groups'), parts along dimension 0, may hold values from 0 to 15, each once
- adapter_rank_used: int32 [32], P('groups'), parts along dimension 0, may hold values from 4 to 16, as said below
- adapter_down_factor: float32 [32, 48, 8192], P(('groups', 'pool')), parts along dimension 0, may hold values from -0.0625 to 0.0625
- query_up_factor: float32 [32, 16, 8192], P(('groups', 'pool')), parts along dimension 0, may hold values from -1.5 to 1.5
- key_value_up_factor: float32 [32, 2, 16, 1024], P(('groups', 'pool')), parts along dimension 0, may hold values from -1.5 to 1.5
- output_down_factor: float32 [32, 16, 8192], P(('groups', 'pool')), parts along dimension 0, may hold values from -0.0625 to 0.0625
- output_up_factor: float32 [32, 16, 8192], P(('groups', 'pool')), parts along dimension 0, may hold values from -1.5 to 1.5
Outputs:
- block_out: bfloat16 [2, 32, 8192], P(None, 'groups', 'pool'), parts along dimension 1
- new_kv: bfloat16 [2, 32, 2048], P(None, ('groups', 'pool')), parts along dimension 1
The draws below stay inside these ranges and needn't reach their ends.
There are 2 independent parts, one for each index of `groups`. The reference program is written for one: setup_inputs(seed, part) draws one part's arguments, and reference() takes and returns one part's arrays. A program takes and returns all parts, laid end to end along the dimension named above; an argument that names none is the same for every part. Nothing has to cross between parts.
Inputs may be any that keep to these rules, and one draw needn't show every extreme that they name: `cache_valid_length`: one request in every draw has all 256 positions valid. `adapter_rank_used`: factor rows at or beyond an adapter's rank are not used; some adapter has rank 16.
All inputs are finite; a program needn't handle non-finite values.
Results may differ from the reference program's by a relative error of at most 0.012.
The reference program's roundings to bfloat16 on the way count: a program that leaves them out, or rounds other values in their place, can miss the bound.
Values may be sent and summed in bfloat16 or wider, within the bound.
A program may use at most 128 MiB of HBM per device.

```python
import jax
import jax.numpy as jnp
from jax import lax

MODEL_WIDTH = 8192
HEADS = 64
KV_HEADS = 8
HEAD_DIM = 128
LARGEST_RANK = 16
STEPS = 2
CACHE = 256
QUERY_FEATURES = 8192
KEY_FEATURES = 1024
REPLICA_ADAPTERS = 16
REQ = 16


def draw_key_value_cache(key, part):
    key = jax.random.fold_in(key, 11)
    first = jax.random.fold_in(key, 0)
    array_shape = (REQ, CACHE, 2 * KV_HEADS * HEAD_DIM)
    values = jnp.clip(jax.random.normal(first, array_shape, jnp.float32), -5.0, 5.0)
    return values.astype(jnp.bfloat16)


def draw_cache_valid_length(key, part):
    key = jax.random.fold_in(key, 12)
    first, second = jax.random.split(key)
    lengths = jax.random.randint(first, (REQ,), 1, CACHE + 1, dtype=jnp.int32)
    chosen = jax.random.randint(second, (), 0, REQ, dtype=jnp.int32)
    return jnp.where(jnp.arange(REQ, dtype=jnp.int32) == chosen, CACHE, lengths).astype(jnp.int32)


def draw_adapter_rank_used(key, part):
    key = jax.random.fold_in(key, 13)
    first, second = jax.random.split(key)
    ranks = jax.random.randint(first, (REPLICA_ADAPTERS,), 4, LARGEST_RANK + 1, dtype=jnp.int32)
    chosen = jax.random.randint(second, (), 0, REPLICA_ADAPTERS, dtype=jnp.int32)
    places = jnp.arange(REPLICA_ADAPTERS, dtype=jnp.int32)
    ranks = jnp.where(places == chosen, LARGEST_RANK, ranks)
    ranks = jnp.where(places == (chosen + 1) % REPLICA_ADAPTERS, 4, ranks)
    return ranks.astype(jnp.int32)


def block_scale(rng, shape, cuts, smallest, largest):
    factor_of = 1.0
    for axis_at, shards_of in cuts:
        heights = jax.random.uniform(jax.random.fold_in(jax.random.fold_in(rng, 6), axis_at), (shards_of,), jnp.float32, smallest / len(cuts), largest / len(cuts))
        factor_of = factor_of * jnp.repeat(jnp.exp(heights), shape[axis_at] // shards_of).reshape((-1,) + (1,) * (len(shape) - 1 - axis_at))
    return factor_of


def distinct(own_key, rows, amount, top, lift):
    sequence = jax.random.permutation(jax.random.fold_in(own_key, 1), amount)
    pull = sequence
    for power in range(3):
        pull = pull * pull // amount
    pull = pull * lift // amount
    chance = jax.random.randint(jax.random.fold_in(own_key, 2), (rows, amount), 0, 4096) + pull
    holders = jax.random.permutation(jax.random.fold_in(own_key, 3), rows)[jnp.arange(amount) % rows]
    chance = jnp.where(jnp.arange(rows)[:, None] == holders[None, :], 1 << 14, chance)
    priority = chance * amount + jnp.arange(amount)
    return lax.top_k(priority.astype(jnp.int32), top)[1].astype(jnp.int32)


def noise(stream_key, shape, deviation, bound, pieces=(), held_as=jnp.bfloat16):
    array = deviation * jax.random.normal(stream_key, shape, jnp.float32)
    if pieces:
        array = array * block_scale(stream_key, shape, pieces, -0.22, 0.18)
    return jnp.clip(array, -bound, bound).astype(held_as)


def setup_inputs(seed: int = 0, part: int = 0) -> dict:
    seeds = jax.random.split(jax.random.key(seed), 15)
    own_keys = jax.random.split(jax.random.fold_in(seeds[14], part), 15)
    return {
        "hidden": noise(own_keys[0], (STEPS, REQ, MODEL_WIDTH), 1.0, 6.0, ((2, 16),)),
        "norm_gain_vector": jnp.clip(1.0 + 0.18 * jax.random.normal(seeds[1], (MODEL_WIDTH,), jnp.float32), 0.1, 1.9),
        "query_key_value_weight": noise(seeds[2], (MODEL_WIDTH, QUERY_FEATURES + 2 * KEY_FEATURES), MODEL_WIDTH ** -0.5, 0.0625, ((0, 16),)),
        "output_weight": noise(seeds[3], (QUERY_FEATURES, MODEL_WIDTH), QUERY_FEATURES ** -0.5, 0.0625, ((1, 16),)),
        "key_value_cache": draw_key_value_cache(jax.random.fold_in(jax.random.fold_in(seeds[14], part), 71), part),
        "cache_valid_length": draw_cache_valid_length(jax.random.fold_in(jax.random.fold_in(seeds[14], part), 71), part),
        "request_adapter_index": distinct(own_keys[6], STEPS * REQ, REPLICA_ADAPTERS, 1, 1024).reshape((STEPS, REQ, 1)),
        "adapter_slot_place": jax.random.permutation(own_keys[7], REPLICA_ADAPTERS).astype(jnp.int32),
        "adapter_rank_used": draw_adapter_rank_used(jax.random.fold_in(jax.random.fold_in(seeds[14], part), 71), part),
        "adapter_down_factor": noise(own_keys[9], (REPLICA_ADAPTERS, 3 * LARGEST_RANK, MODEL_WIDTH), MODEL_WIDTH ** -0.5, 0.0625, ((0, 16),), jnp.float32),
        "query_up_factor": noise(own_keys[10], (REPLICA_ADAPTERS, LARGEST_RANK, QUERY_FEATURES), LARGEST_RANK ** -0.5, 1.5, ((0, 16),), jnp.float32),
        "key_value_up_factor": noise(own_keys[11], (REPLICA_ADAPTERS, 2, LARGEST_RANK, KEY_FEATURES), LARGEST_RANK ** -0.5, 1.5, ((0, 16),), jnp.float32),
        "output_down_factor": noise(own_keys[12], (REPLICA_ADAPTERS, LARGEST_RANK, QUERY_FEATURES), QUERY_FEATURES ** -0.5, 0.0625, ((0, 16),), jnp.float32),
        "output_up_factor": noise(own_keys[13], (REPLICA_ADAPTERS, LARGEST_RANK, MODEL_WIDTH), LARGEST_RANK ** -0.5, 1.5, ((0, 16),), jnp.float32),
    }


epsilon = 1e-05
highest_precision = lax.Precision.HIGHEST

def lookup(lookup_table, lookup_index):
    matches = lookup_index[:, None] == jnp.arange(lookup_table.shape[0], dtype=jnp.int32)[None, :]
    return lax.optimization_barrier(jnp.sum(jnp.where(matches, lookup_table[None, :], 0), axis=1)).astype(jnp.int32)

def widen_rows(slot_onehot, shrunk_rows, factors):
    spread = (slot_onehot[:, :, None] * shrunk_rows[:, None, :]).reshape(slot_onehot.shape[0], -1)
    return jnp.dot(spread, factors.reshape(spread.shape[1], factors.shape[-1]), precision=highest_precision)

def attend_one(queries, cache_rows, length, fresh_kv):
    kv_width = KV_HEADS * HEAD_DIM
    group_size = HEADS // KV_HEADS
    score_scale = HEAD_DIM ** (-0.5)
    keys_cache = cache_rows[:, :kv_width].astype(jnp.float32).reshape(CACHE, KV_HEADS, HEAD_DIM)
    values_cache = cache_rows[:, kv_width:].astype(jnp.float32).reshape(CACHE, KV_HEADS, HEAD_DIM)
    keys_fresh = fresh_kv[:, :kv_width].astype(jnp.float32).reshape(-1, KV_HEADS, HEAD_DIM)
    values_fresh = fresh_kv[:, kv_width:].astype(jnp.float32).reshape(-1, KV_HEADS, HEAD_DIM)
    query_heads = queries.astype(jnp.float32).reshape(KV_HEADS, group_size, HEAD_DIM)
    cache_scores = jnp.einsum('hgd,chd->hgc', query_heads, keys_cache, precision=highest_precision) * score_scale
    valid_cache = jnp.arange(CACHE) < length
    cache_scores = jnp.where(valid_cache[None, None, :], cache_scores, -1e+30)
    fresh_scores = jnp.einsum('hgd,nhd->hgn', query_heads, keys_fresh, precision=highest_precision) * score_scale
    row_max = jnp.maximum(lax.optimization_barrier(jnp.max(cache_scores, axis=-1)), lax.optimization_barrier(jnp.max(fresh_scores, axis=-1)))
    cache_exp = jnp.exp(cache_scores - row_max[:, :, None])
    fresh_exp = jnp.exp(fresh_scores - row_max[:, :, None])
    total = lax.optimization_barrier(jnp.sum(cache_exp, axis=-1)) + lax.optimization_barrier(jnp.sum(fresh_exp, axis=-1))
    cache_weights = (cache_exp / total[:, :, None]).astype(jnp.bfloat16).astype(jnp.float32)
    fresh_weights = (fresh_exp / total[:, :, None]).astype(jnp.bfloat16).astype(jnp.float32)
    result = jnp.einsum('hgc,chd->hgd', cache_weights, values_cache, precision=highest_precision)
    result = result + jnp.einsum('hgn,nhd->hgd', fresh_weights, values_fresh, precision=highest_precision)
    return result.reshape(HEADS * HEAD_DIM).astype(jnp.bfloat16)

def reference(hidden, norm_gain_vector, query_key_value_weight, output_weight, key_value_cache, cache_valid_length, request_adapter_index, adapter_slot_place, adapter_rank_used, adapter_down_factor, query_up_factor, key_value_up_factor, output_down_factor, output_up_factor):
    query_feature_width = HEADS * HEAD_DIM
    outputs = []
    entries = []
    for step_index in range(STEPS):
        adapter_of = request_adapter_index[step_index, :, 0]
        slot_of = lookup(adapter_slot_place, adapter_of)
        rank_of = lookup(adapter_rank_used, adapter_of)
        factor = 4.0 / jnp.sqrt(rank_of.astype(jnp.float32))
        rank_keep = (jnp.arange(LARGEST_RANK)[None, :] < rank_of[:, None]).astype(jnp.float32) * factor[:, None]
        slot_onehot = (slot_of[:, None] == jnp.arange(REPLICA_ADAPTERS)[None, :]).astype(jnp.float32)
        rows_in = hidden[step_index].astype(jnp.float32)
        inverse = lax.rsqrt(lax.optimization_barrier(jnp.mean(rows_in * rows_in, axis=1)) + epsilon)
        scaled_rows = rows_in * norm_gain_vector[None, :]
        normed = (scaled_rows * inverse[:, None]).astype(jnp.bfloat16)
        gathered_everywhere = jnp.dot(scaled_rows, adapter_down_factor.reshape(REPLICA_ADAPTERS * 3 * LARGEST_RANK, MODEL_WIDTH).T, precision=highest_precision)
        gathered_everywhere = gathered_everywhere.reshape(REQ, REPLICA_ADAPTERS, 3 * LARGEST_RANK)
        shrunk_rows = lax.optimization_barrier(jnp.sum(slot_onehot[:, :, None] * gathered_everywhere, axis=1)) * inverse[:, None]
        shrunk_rows = shrunk_rows.reshape(REQ, 3, LARGEST_RANK) * rank_keep[:, None, :]
        query_update = widen_rows(slot_onehot, shrunk_rows[:, 0], query_up_factor)
        key_update = widen_rows(slot_onehot, shrunk_rows[:, 1], key_value_up_factor[:, 0])
        value_update = widen_rows(slot_onehot, shrunk_rows[:, 2], key_value_up_factor[:, 1])
        mixed = jnp.dot(normed, query_key_value_weight, preferred_element_type=jnp.float32)
        mixed = mixed + jnp.concatenate([query_update, key_update, value_update], axis=1)
        queries = mixed[:, :query_feature_width].astype(jnp.bfloat16)
        kv_entry = mixed[:, query_feature_width:].astype(jnp.bfloat16)
        entries.append(kv_entry)
        fresh_kv = jnp.stack(entries, axis=1)
        attention_result = lax.map(lambda packed: attend_one(*packed), (queries, key_value_cache, cache_valid_length, fresh_kv))
        base_out = jnp.dot(attention_result, output_weight, preferred_element_type=jnp.float32)
        gathered_output_everywhere = jnp.dot(attention_result.astype(jnp.float32), output_down_factor.reshape(REPLICA_ADAPTERS * LARGEST_RANK, query_feature_width).T, precision=highest_precision)
        gathered_output_everywhere = gathered_output_everywhere.reshape(REQ, REPLICA_ADAPTERS, LARGEST_RANK)
        output_shrink_rows = lax.optimization_barrier(jnp.sum(slot_onehot[:, :, None] * gathered_output_everywhere, axis=1)) * rank_keep
        output_update = widen_rows(slot_onehot, output_shrink_rows, output_up_factor)
        outputs.append((rows_in + base_out + output_update).astype(jnp.bfloat16))
    return (jnp.stack(outputs), jnp.stack(entries))
```

```python
import functools

import jax
import jax.numpy as jnp
from jax import lax
from jax.experimental import pallas as pl
from jax.experimental.pallas import tpu as pltpu
from jax.sharding import PartitionSpec as P

HEADS = 64
KV_HEADS = 8
HEAD_DIM = 128
GROUP = HEADS // KV_HEADS
STEPS = 2
RANK = 16
LANES = 128
CHUNK = 2 * KV_HEADS * HEAD_DIM
QUERY_CHUNKS = HEADS * HEAD_DIM // CHUNK
CHUNKS = QUERY_CHUNKS + 1
CHUNK_HEADS = CHUNK // HEAD_DIM
PACKED = CHUNK_HEADS * STEPS

epsilon = 1e-05
f32, bf16 = jnp.float32, jnp.bfloat16


def dot(a, b):
    return jnp.dot(a, b, preferred_element_type=f32)


def dot_t(a, b):
    return lax.dot_general(a, b, (((1,), (1,)), ((), ())), preferred_element_type=f32)


def split(a):
    high = a.astype(bf16)
    return high, (a - high.astype(f32)).astype(bf16)


def kernel(
    n,
    width,
    hid_ref,
    gain_ref,
    length_ref,
    index_ref,
    place_ref,
    rank_ref,
    wqkv_hbm,
    wout_hbm,
    cache_hbm,
    down_hbm,
    qup_hbm,
    kvup_hbm,
    odown_hbm,
    oup_hbm,
    out_ref,
    newkv_ref,
    wqkv,
    wout,
    cache,
    down,
    qup,
    kvup,
    odown,
    oup,
    down_split,
    odown_split,
    hid_all,
    normed_ref,
    part,
    core_out,
    core_in,
    half,
    y_out,
    y_in,
    quarter,
    z_rows,
    z_out,
    z_in,
    kv_rows,
    kv_flat,
    att_all,
    att_rows,
    att,
    oup_out,
    oup_in,
    small,
    load_sem,
    hid_send,
    hid_recv,
    att_send,
    att_recv,
    core_send,
    core_recv,
    y_send,
    y_recv,
    z_send,
    z_recv,
    oup_send,
    oup_recv,
    small_send,
    small_recv,
):
    me = lax.axis_index("pool")
    depth = n // 4
    my_z, my_y, my_core = me // 4, lax.rem(me // 2, 2), lax.rem(me, 2)
    rows = STEPS * n
    wd = width // n

    def at(z, y, core):
        return z * 4 + y * 2 + core

    core_peer = at(my_z, my_y, 1 - my_core)
    y_peer = at(my_z, 1 - my_y, my_core)

    def push(src, dst, send, recv, peer):
        return pltpu.make_async_remote_copy(
            src_ref=src,
            dst_ref=dst,
            send_sem=send,
            recv_sem=recv,
            device_id={"pool": peer},
            device_id_type=pl.DeviceIdType.MESH,
        )

    order = [QUERY_CHUNKS] + list(range(QUERY_CHUNKS))
    loads = [
        (down_hbm, down),
        (odown_hbm, odown),
        (oup_hbm, oup),
        (qup_hbm, qup),
        (kvup_hbm, kvup),
    ]
    loads += [(wqkv_hbm.at[:, pl.ds(c * CHUNK, CHUNK)], wqkv.at[c]) for c in order]
    loads += [(cache_hbm, cache), (wout_hbm, wout)]
    loads = [pltpu.make_async_copy(s, d, load_sem.at[i]) for i, (s, d) in enumerate(loads)]
    for load in loads:
        load.start()
    load_w = dict(zip(order, loads[5:]))
    load_cache, load_wout = loads[-2:]

    barrier = pltpu.get_barrier_semaphore()

    def greet(k, carry):
        pl.semaphore_signal(
            barrier,
            inc=1,
            device_id={"pool": lax.rem(me + k, n)},
            device_id_type=pl.DeviceIdType.MESH,
        )
        return carry

    lax.fori_loop(1, n, greet, 0)

    row = lax.broadcasted_iota(jnp.int32, (rows, rows), 0)
    column = lax.broadcasted_iota(jnp.int32, (rows, rows), 1)
    z_bits = depth.bit_length() - 1
    source = (
        (row & (STEPS - 1)) * n
        + ((row >> 1) & (depth - 1)) * 4
        + ((row >> (1 + z_bits)) & 1) * 2
        + (row >> (2 + z_bits))
    )
    order_rows = (source == column).astype(f32)
    hid_all[me] = dot(order_rows.astype(bf16), hid_ref[...]).astype(bf16)

    lane = lax.broadcasted_iota(jnp.int32, (rows, LANES), 1)
    adapters = place_ref.shape[1]
    matches = index_ref[...] == lax.broadcasted_iota(jnp.int32, (rows, adapters), 1)
    slot_of = jnp.sum(jnp.where(matches, place_ref[...].astype(f32), 0.0), axis=1, keepdims=True)
    rank_of = jnp.sum(jnp.where(matches, rank_ref[...].astype(f32), 0.0), axis=1, keepdims=True)
    keep = jnp.where(lane.astype(f32) < rank_of, 4.0 / jnp.sqrt(rank_of), 0.0)
    own_keep = jnp.where(slot_of == me.astype(f32), keep, 0.0)
    own_keep_ordered = jnp.dot(
        order_rows, own_keep, precision=lax.Precision.HIGHEST, preferred_element_type=f32
    )

    pl.semaphore_wait(barrier, n - 1)

    def gather(buffer, send, recv, use):
        started = []

        def start(block, peer):
            copy = push(buffer.at[block], buffer.at[block], send.at[len(started)], recv.at[block], peer)
            copy.start()
            started.append(copy)

        def arrived(block):
            push(buffer.at[block], buffer.at[block], send.at[0], recv.at[block], core_peer).wait_recv()

        for k in range(1, depth):
            start(me, at(lax.rem(my_z + k, depth), my_y, my_core))
        start(me, y_peer)
        start(me, core_peer)
        yield
        use(me)
        for k in range(1, depth):
            block = at(lax.rem(my_z + k, depth), my_y, my_core)
            arrived(block)
            start(block, y_peer)
            start(block, core_peer)
            use(block)
        for k in range(depth):
            block = at(lax.rem(my_z + k, depth), 1 - my_y, my_core)
            arrived(block)
            start(block, core_peer)
            use(block)
        for y in (my_y, 1 - my_y):
            for k in range(depth):
                block = at(lax.rem(my_z + k, depth), y, 1 - my_core)
                arrived(block)
                use(block)
        yield
        for copy in started:
            copy.wait_send()

    totals = [jnp.zeros((rows, 1), f32), jnp.zeros((rows, LANES), f32)]

    def use_hidden(block):
        values = hid_all[block]
        wide = values.astype(f32)
        totals[0] += jnp.sum(wide * wide, axis=1, keepdims=True)
        columns = pl.ds(pl.multiple_of(block * wd, wd), wd)
        totals[1] += dot_t(values, down_split[:, columns])

    hidden_gather = gather(hid_all, hid_send, hid_recv, use_hidden)
    next(hidden_gather)

    lora_rows = 3 * RANK
    down_split[2 * lora_rows :, :] = jnp.zeros((LANES - 2 * lora_rows, width), bf16)
    odown_split[2 * RANK :, :] = jnp.zeros((LANES - 2 * RANK, width), bf16)
    loads[0].wait()
    for start in range(0, width, 1024):
        columns = pl.ds(start, 1024)
        high, low = split(down[:, columns] * gain_ref[:, columns])
        down_split[:lora_rows, columns] = high
        down_split[lora_rows : 2 * lora_rows, columns] = low

    next(hidden_gather)

    loads[1].wait()
    loads[2].wait()
    for p in range(n):
        oup_out[p] = oup[:, p * wd : (p + 1) * wd].astype(bf16)
    mine = pl.ds(pl.multiple_of(me * RANK, RANK), RANK)
    oup_in[mine, :] = oup_out[me]

    def oup_copy(k):
        peer = lax.rem(me + k, n)
        return push(oup_out.at[peer], oup_in.at[mine, :], oup_send.at[k], oup_recv.at[me], peer)

    def start_oup(k, carry):
        oup_copy(k).start()
        return carry

    lax.fori_loop(1, n, start_oup, 0)

    inverse = lax.rsqrt(totals[0] * (1.0 / width) + epsilon)
    shrink = (totals[1] + pltpu.roll(totals[1], LANES - lora_rows, 1)) * inverse
    shrink_q = split((shrink * own_keep_ordered)[:, :RANK])
    shrink_k = split((pltpu.roll(shrink, LANES - RANK, 1) * own_keep_ordered)[:, :RANK])
    shrink_v = split((pltpu.roll(shrink, LANES - 2 * RANK, 1) * own_keep_ordered)[:, :RANK])
    gain_mine = gain_ref[:, pl.ds(pl.multiple_of(me * wd, wd), wd)]
    normed_ref[...] = (hid_all[me].astype(f32) * gain_mine * inverse).astype(bf16)
    loads[3].wait()
    loads[4].wait()

    def widen(shrunk, factors):
        high, low = split(factors)
        return dot(shrunk[0], high) + dot(shrunk[1], high) + dot(shrunk[0], low)

    rows_core, rows_y = rows // 2, rows // 4
    half_chunk = CHUNK // 2

    def core_copy(c):
        return push(core_out.at[c], core_in.at[c], core_send.at[c], core_recv.at[c], core_peer)

    def y_copy(c):
        return push(y_out.at[c], y_in.at[c], y_send.at[c], y_recv.at[c], y_peer)

    def z_copy(c, k):
        z = lax.rem(my_z + k, depth)
        return push(
            z_out.at[c, z],
            z_in.at[c, my_z],
            z_send.at[c, k],
            z_recv.at[c, my_z],
            at(z, my_y, my_core),
        )

    def project(c):
        load_w[c].wait()
        if c < QUERY_CHUNKS:
            lora = [(shrink_q, qup[:, c * CHUNK : (c + 1) * CHUNK], 0, CHUNK)]
        else:
            lora = [(shrink_k, kvup[0], 0, half_chunk), (shrink_v, kvup[1], half_chunk, half_chunk)]
        for shrunk, factors, first, size in lora:
            part[c, :, first : first + size] = dot(
                normed_ref[...], wqkv[c, :, first : first + size]
            ) + widen(shrunk, factors)
        other = pl.ds(pl.multiple_of((1 - my_core) * rows_core, rows_core), rows_core)
        core_out[c] = part[c, other, :].astype(bf16)
        core_copy(c).start()

    def add_core(c):
        core_copy(c).wait_recv()
        own = pl.ds(pl.multiple_of(my_core * rows_core, rows_core), rows_core)
        half[c] = part[c, own, :] + core_in[c].astype(f32)
        other = half[c, pl.ds(pl.multiple_of((1 - my_y) * rows_y, rows_y), rows_y), :]
        y_out[c] = jnp.concatenate([other[:, :half_chunk], other[:, half_chunk:]], axis=0).astype(bf16)
        y_copy(c).start()

    def add_y(c):
        y_copy(c).wait_recv()
        own = half[c, pl.ds(pl.multiple_of(my_y * rows_y, rows_y), rows_y), :]
        arrived = y_in[c].astype(f32)
        quarter[c, :, :half_chunk] = own[:, :half_chunk] + arrived[:rows_y]
        quarter[c, :, half_chunk:] = own[:, half_chunk:] + arrived[rows_y:]
        for z in range(depth):
            for j in range(CHUNK_HEADS):
                z_rows[c, z, STEPS * j : STEPS * (j + 1), :] = quarter[
                    c, STEPS * z : STEPS * (z + 1), HEAD_DIM * j : HEAD_DIM * (j + 1)
                ]
        z_out[c] = z_rows[c].astype(bf16)
        for k in range(1, depth):
            z_copy(c, k).start()

    def add_z(c):
        total = z_rows[c, my_z]
        for k in range(1, depth):
            z = lax.rem(my_z + k, depth)
            push(
                z_out.at[c, z], z_in.at[c, z], z_send.at[c, k], z_recv.at[c, z], core_peer
            ).wait_recv()
            total += z_in[c, z].astype(f32)
        return total.astype(bf16)

    for step in range(CHUNKS + 2):
        if step < CHUNKS:
            project(order[step])
        if 0 <= step - 1 < CHUNKS:
            add_core(order[step - 1])
        if 0 <= step - 2 < CHUNKS:
            add_y(order[step - 2])

    for start in range(0, width, 1024):
        columns = pl.ds(start, 1024)
        high, low = split(odown[:, columns])
        odown_split[:RANK, columns] = high
        odown_split[RANK : 2 * RANK, columns] = low

    load_cache.wait()
    kv_rows[...] = add_z(QUERY_CHUNKS).astype(f32)
    group_rows = GROUP * STEPS
    positions = cache.shape[0]
    scale = HEAD_DIM ** (-0.5)
    valid = lax.broadcasted_iota(jnp.int32, (group_rows, positions), 1) < length_ref[...]
    first_step = (lax.broadcasted_iota(jnp.int32, (group_rows, 1), 0) & (STEPS - 1)) == 0
    kv_width = KV_HEADS * HEAD_DIM
    for c in range(QUERY_CHUNKS):
        queries_all = add_z(c)
        for g in range(CHUNK_HEADS // GROUP):
            head = c * (CHUNK_HEADS // GROUP) + g
            queries = queries_all[g * group_rows : (g + 1) * group_rows]
            columns = slice(head * HEAD_DIM, (head + 1) * HEAD_DIM)
            value_columns = slice(kv_width + head * HEAD_DIM, kv_width + (head + 1) * HEAD_DIM)
            keys = [kv_rows[STEPS * head + t : STEPS * head + t + 1, :] for t in range(STEPS)]
            fresh_at = STEPS * (KV_HEADS + head)
            values = [kv_rows[fresh_at + t : fresh_at + t + 1, :] for t in range(STEPS)]
            scores = jnp.where(valid, dot_t(queries, cache[:, columns]) * scale, -1e30)
            wide = queries.astype(f32)
            fresh = [jnp.sum(wide * key, axis=1, keepdims=True) * scale for key in keys]
            fresh[1] = jnp.where(first_step, -1e30, fresh[1])
            top = jnp.maximum(jnp.max(scores, axis=1, keepdims=True), jnp.maximum(*fresh))
            exps = jnp.exp(scores - top)
            fresh = [jnp.exp(s - top) for s in fresh]
            total = jnp.sum(exps, axis=1, keepdims=True) + fresh[0] + fresh[1]
            result = dot((exps / total).astype(bf16), cache[:, value_columns])
            for s, value in zip(fresh, values):
                result += (s / total).astype(bf16).astype(f32) * value
            att_all[me, pl.ds(head * group_rows, group_rows), :] = result.astype(bf16)

    att_block = HEADS * STEPS

    def use_attended(block):
        att_rows[pl.ds(pl.multiple_of(block * att_block, att_block), att_block), :] = att_all[
            block
        ].astype(f32)

    attended_gather = gather(att_all, att_send, att_recv, use_attended)
    next(attended_gather)
    for t in range(STEPS):
        for j in range(CHUNK_HEADS):
            kv_flat[t : t + 1, HEAD_DIM * j : HEAD_DIM * (j + 1)] = kv_rows[
                STEPS * j + t : STEPS * j + t + 1, :
            ]
    newkv_ref[...] = kv_flat[...].astype(bf16)
    next(attended_gather)

    for h in range(HEADS):
        for t in range(STEPS):
            att[t * n : (t + 1) * n, h * HEAD_DIM : (h + 1) * HEAD_DIM] = att_rows[
                pl.ds(STEPS * h + t, n, stride=att_block), :
            ].astype(bf16)

    shrunk = dot_t(att[...], odown_split[...])
    shrunk = (shrunk + pltpu.roll(shrunk, LANES - RANK, 1)) * own_keep
    spots = LANES // RANK
    packed = []
    for q in range(max(1, rows // (8 * spots))):
        groups = min(spots, rows // 8 - q * spots)
        total = jnp.zeros((8, LANES), f32)
        for g in range(groups):
            first = 8 * (q * spots + g)
            piece = shrunk[first : first + 8]
            total += piece if g == 0 else pltpu.roll(piece, RANK * g, 1)
        packed.append(total)
    small[me] = packed[0] if len(packed) == 1 else jnp.concatenate(packed, axis=0)

    def small_copy(k):
        peer = lax.rem(me + k, n)
        return push(small.at[me], small.at[me], small_send.at[k], small_recv.at[me], peer)

    def start_small(k, carry):
        small_copy(k).start()
        return carry

    lax.fori_loop(1, n, start_small, 0)

    load_wout.wait()
    base = dot(att[...], wout[...]) + hid_ref[...].astype(f32)

    def end_oup(k, carry):
        other = lax.rem(me + k, n)
        theirs = pl.ds(pl.multiple_of(other * RANK, RANK), RANK)
        push(
            oup_out.at[other], oup_in.at[theirs, :], oup_send.at[k], oup_recv.at[other], other
        ).wait()
        return carry

    lax.fori_loop(1, n, end_oup, 0)

    def end_small(k, carry):
        other = lax.rem(me + k, n)
        push(small.at[other], small.at[other], small_send.at[k], small_recv.at[other], other).wait()
        return carry

    lax.fori_loop(1, n, end_small, 0)

    whole = small[0]
    for p in range(1, n):
        whole += small[p]
    pieces = []
    for i in range(rows // 8):
        q, g = divmod(i, spots)
        piece = whole[8 * q : 8 * q + 8]
        pieces.append(piece if g == 0 else pltpu.roll(piece, LANES - RANK * g, 1))
    rows_out = jnp.where(lane < RANK, jnp.concatenate(pieces, axis=0), 0.0)
    reach = RANK
    while reach < LANES:
        rows_out += pltpu.roll(rows_out, reach, 1)
        reach *= 2
    spread = jnp.concatenate([rows_out] * (n * RANK // LANES), axis=1)
    place_of = lax.broadcasted_iota(jnp.int32, (rows, n * RANK), 1) >> (RANK.bit_length() - 1)
    high, low = split(jnp.where(place_of.astype(f32) == slot_of, spread, 0.0))
    update = dot(high, oup_in[...]) + dot(low, oup_in[...])
    out_ref[...] = (base + update).astype(bf16)

    for gathered in (hidden_gather, attended_gather):
        for _ in gathered:
            pass
    for c in range(CHUNKS):
        core_copy(c).wait_send()
        y_copy(c).wait_send()
        for k in range(1, depth):
            z_copy(c, k).wait_send()


def local(
    n,
    hidden,
    norm_gain_vector,
    query_key_value_weight,
    output_weight,
    key_value_cache,
    cache_valid_length,
    request_adapter_index,
    adapter_slot_place,
    adapter_rank_used,
    adapter_down_factor,
    query_up_factor,
    key_value_up_factor,
    output_down_factor,
    output_up_factor,
):
    steps, requests, wd = hidden.shape
    width = norm_gain_vector.shape[0]
    positions = key_value_cache.shape[1]
    assert steps == STEPS and requests == n and adapter_down_factor.shape[0] == 1 and wd * n == width
    rows, depth = steps * n, n // 4
    att_block = HEADS * STEPS
    sends = 4 * depth
    packed_rows = 8 * max(1, rows * RANK // (8 * LANES))
    vmem = pl.BlockSpec(memory_space=pltpu.VMEM)
    hbm = pl.BlockSpec(memory_space=pl.ANY)
    dma = pltpu.SemaphoreType.DMA
    out, new_kv = pl.pallas_call(
        functools.partial(kernel, n, width),
        out_shape=(
            jax.ShapeDtypeStruct((rows, wd), bf16),
            jax.ShapeDtypeStruct((STEPS, CHUNK), bf16),
        ),
        in_specs=[vmem] * 6 + [hbm] * 8,
        out_specs=(vmem, vmem),
        scratch_shapes=[
            pltpu.VMEM((CHUNKS, wd, CHUNK), bf16),
            pltpu.VMEM((width, wd), bf16),
            pltpu.VMEM((positions, CHUNK), bf16),
            pltpu.VMEM((3 * RANK, width), f32),
            pltpu.VMEM((RANK, width), f32),
            pltpu.VMEM((2, RANK, CHUNK // 2), f32),
            pltpu.VMEM((RANK, width), f32),
            pltpu.VMEM((RANK, width), f32),
            pltpu.VMEM((LANES, width), bf16),
            pltpu.VMEM((LANES, width), bf16),
            pltpu.VMEM((n, rows, wd), bf16),
            pltpu.VMEM((rows, wd), bf16),
            pltpu.VMEM((CHUNKS, rows, CHUNK), f32),
            pltpu.VMEM((CHUNKS, rows // 2, CHUNK), bf16),
            pltpu.VMEM((CHUNKS, rows // 2, CHUNK), bf16),
            pltpu.VMEM((CHUNKS, rows // 2, CHUNK), f32),
            pltpu.VMEM((CHUNKS, rows // 2, CHUNK // 2), bf16),
            pltpu.VMEM((CHUNKS, rows // 2, CHUNK // 2), bf16),
            pltpu.VMEM((CHUNKS, rows // 4, CHUNK), f32),
            pltpu.VMEM((CHUNKS, depth, PACKED, HEAD_DIM), f32),
            pltpu.VMEM((CHUNKS, depth, PACKED, HEAD_DIM), bf16),
            pltpu.VMEM((CHUNKS, depth, PACKED, HEAD_DIM), bf16),
            pltpu.VMEM((PACKED, HEAD_DIM), f32),
            pltpu.VMEM((STEPS, CHUNK), f32),
            pltpu.VMEM((n, att_block, HEAD_DIM), bf16),
            pltpu.VMEM((n * att_block, HEAD_DIM), f32),
            pltpu.VMEM((rows, HEADS * HEAD_DIM), bf16),
            pltpu.VMEM((n, RANK, wd), bf16),
            pltpu.VMEM((n * RANK, wd), bf16),
            pltpu.VMEM((n, packed_rows, LANES), f32),
            dma((5 + CHUNKS + 2,)),
            dma((sends,)),
            dma((n,)),
            dma((sends,)),
            dma((n,)),
            dma((CHUNKS,)),
            dma((CHUNKS,)),
            dma((CHUNKS,)),
            dma((CHUNKS,)),
            dma((CHUNKS, depth)),
            dma((CHUNKS, depth)),
            dma((n,)),
            dma((n,)),
            dma((n,)),
            dma((n,)),
        ],
        compiler_params=pltpu.CompilerParams(
            collective_id=0, has_side_effects=True, vmem_limit_bytes=56 * 1024 * 1024
        ),
        cost_estimate=pl.CostEstimate(
            flops=2 * rows * 18 * 1024 * width // n * 8, bytes_accessed=24 << 20, transcendentals=0
        ),
    )(
        hidden.reshape(rows, wd),
        norm_gain_vector.reshape(1, width),
        cache_valid_length.reshape(1, 1),
        request_adapter_index.reshape(rows, 1),
        adapter_slot_place.reshape(1, -1),
        adapter_rank_used.reshape(1, -1),
        query_key_value_weight,
        output_weight,
        key_value_cache.reshape(positions, CHUNK),
        adapter_down_factor.reshape(3 * RANK, width),
        query_up_factor.reshape(RANK, width),
        key_value_up_factor.reshape(2, RANK, CHUNK // 2),
        output_down_factor.reshape(RANK, width),
        output_up_factor.reshape(RANK, width),
    )
    return out.reshape(steps, requests, wd), new_kv.reshape(steps, 1, CHUNK)


def solution(mesh):
    placed = (
        P(None, "groups", "pool"),
        P(),
        P("pool", None),
        P(None, "pool"),
        P(("groups", "pool"), None, None),
        P(("groups", "pool")),
        P(None, "groups", None),
        P("groups"),
        P("groups"),
        P(("groups", "pool"), None, None),
        P(("groups", "pool"), None, None),
        P(("groups", "pool"), None, None, None),
        P(("groups", "pool"), None, None),
        P(("groups", "pool"), None, None),
    )
    return jax.shard_map(
        functools.partial(local, mesh.shape["pool"]),
        mesh=mesh,
        in_specs=placed,
        out_specs=(P(None, "groups", "pool"), P(None, ("groups", "pool"), None)),
        check_vma=False,
    )
```

```python
import functools

import jax
import jax.numpy as jnp
from jax import lax
from jax.experimental import pallas as pl
from jax.experimental.pallas import tpu as pltpu
from jax.sharding import PartitionSpec as P

HEADS = 64
KV_HEADS = 8
HEAD_DIM = 128
GROUP = HEADS // KV_HEADS
STEPS = 2
RANK = 16
LANES = 128
CHUNK = 2 * KV_HEADS * HEAD_DIM
QUERY_CHUNKS = HEADS * HEAD_DIM // CHUNK
CHUNKS = QUERY_CHUNKS + 1
CHUNK_HEADS = CHUNK // HEAD_DIM
PACKED = CHUNK_HEADS * STEPS

epsilon = 1e-05
f32, bf16 = jnp.float32, jnp.bfloat16


def dot(a, b):
    return jnp.dot(a, b, preferred_element_type=f32)


def dot_t(a, b):
    return lax.dot_general(a, b, (((1,), (1,)), ((), ())), preferred_element_type=f32)


def split(a):
    high = a.astype(bf16)
    return high, (a - high.astype(f32)).astype(bf16)


def kernel(
    n,
    width,
    hid_ref,
    gain_ref,
    length_ref,
    index_ref,
    place_ref,
    rank_ref,
    wqkv_hbm,
    wout_hbm,
    cache_hbm,
    down_hbm,
    qup_hbm,
    kvup_hbm,
    odown_hbm,
    oup_hbm,
    out_ref,
    newkv_ref,
    wqkv,
    wout,
    cache,
    down,
    qup,
    kvup,
    odown,
    oup,
    down_split,
    odown_split,
    hid_all,
    normed_ref,
    part,
    core_out,
    core_in,
    half,
    y_out,
    y_in,
    quarter,
    z_rows,
    z_out,
    z_in,
    kv_rows,
    kv_flat,
    att_all,
    att_rows,
    att,
    oup_out,
    oup_in,
    small,
    load_sem,
    hid_send,
    hid_recv,
    att_send,
    att_recv,
    core_send,
    core_recv,
    y_send,
    y_recv,
    z_send,
    z_recv,
    oup_send,
    oup_recv,
    small_send,
    small_recv,
):
    me = lax.axis_index("pool")
    depth = n // 4
    my_z, my_y, my_core = me // 4, lax.rem(me // 2, 2), lax.rem(me, 2)
    rows = STEPS * n
    wd = width // n

    def at(z, y, core):
        return z * 4 + y * 2 + core

    core_peer = at(my_z, my_y, 1 - my_core)
    y_peer = at(my_z, 1 - my_y, my_core)

    def push(src, dst, send, recv, peer):
        return pltpu.make_async_remote_copy(
            src_ref=src,
            dst_ref=dst,
            send_sem=send,
            recv_sem=recv,
            device_id={"pool": peer},
            device_id_type=pl.DeviceIdType.MESH,
        )

    order = [QUERY_CHUNKS] + list(range(QUERY_CHUNKS))
    loads = [
        (down_hbm, down),
        (odown_hbm, odown),
        (oup_hbm, oup),
        (qup_hbm, qup),
        (kvup_hbm, kvup),
    ]
    loads += [(wqkv_hbm.at[:, pl.ds(c * CHUNK, CHUNK)], wqkv.at[c]) for c in order]
    loads += [(cache_hbm, cache), (wout_hbm, wout)]
    loads = [pltpu.make_async_copy(s, d, load_sem.at[i]) for i, (s, d) in enumerate(loads)]
    for load in loads:
        load.start()
    load_w = dict(zip(order, loads[5:]))
    load_cache, load_wout = loads[-2:]

    barrier = pltpu.get_barrier_semaphore()

    def greet(k, carry):
        pl.semaphore_signal(
            barrier,
            inc=1,
            device_id={"pool": lax.rem(me + k, n)},
            device_id_type=pl.DeviceIdType.MESH,
        )
        return carry

    lax.fori_loop(1, n, greet, 0)

    row = lax.broadcasted_iota(jnp.int32, (rows, rows), 0)
    column = lax.broadcasted_iota(jnp.int32, (rows, rows), 1)
    z_bits = depth.bit_length() - 1
    source = (
        (row & (STEPS - 1)) * n
        + ((row >> 1) & (depth - 1)) * 4
        + ((row >> (1 + z_bits)) & 1) * 2
        + (row >> (2 + z_bits))
    )
    order_rows = (source == column).astype(f32)
    hid_all[me] = dot(order_rows.astype(bf16), hid_ref[...]).astype(bf16)

    lane = lax.broadcasted_iota(jnp.int32, (rows, LANES), 1)
    adapters = place_ref.shape[1]
    same = lax.broadcasted_iota(jnp.int32, (n, n), 0) == lax.broadcasted_iota(jnp.int32, (n, n), 1)
    adapter_of = jnp.concatenate(
        [
            jnp.sum(jnp.where(same, index_ref[t].astype(f32), 0.0), axis=1, keepdims=True)
            for t in range(STEPS)
        ],
        axis=0,
    )
    adapter = lax.broadcasted_iota(jnp.int32, (rows, adapters), 1)
    matches = adapter_of == adapter.astype(f32)
    slot_of = jnp.sum(jnp.where(matches, place_ref[...].astype(f32), 0.0), axis=1, keepdims=True)
    rank_of = jnp.sum(jnp.where(matches, rank_ref[...].astype(f32), 0.0), axis=1, keepdims=True)
    keep = jnp.where(lane.astype(f32) < rank_of, 4.0 / jnp.sqrt(rank_of), 0.0)
    own_keep = jnp.where(slot_of == me.astype(f32), keep, 0.0)
    own_keep_ordered = jnp.dot(
        order_rows, own_keep, precision=lax.Precision.HIGHEST, preferred_element_type=f32
    )

    pl.semaphore_wait(barrier, n - 1)

    def gather(buffer, send, recv, use):
        started = []

        def start(block, peer):
            copy = push(buffer.at[block], buffer.at[block], send.at[len(started)], recv.at[block], peer)
            copy.start()
            started.append(copy)

        def arrived(block):
            push(buffer.at[block], buffer.at[block], send.at[0], recv.at[block], core_peer).wait_recv()

        for k in range(1, depth):
            start(me, at(lax.rem(my_z + k, depth), my_y, my_core))
        start(me, y_peer)
        start(me, core_peer)
        yield
        use(me)
        for k in range(1, depth):
            block = at(lax.rem(my_z + k, depth), my_y, my_core)
            arrived(block)
            start(block, y_peer)
            start(block, core_peer)
            use(block)
        for k in range(depth):
            block = at(lax.rem(my_z + k, depth), 1 - my_y, my_core)
            arrived(block)
            start(block, core_peer)
            use(block)
        for y in (my_y, 1 - my_y):
            for k in range(depth):
                block = at(lax.rem(my_z + k, depth), y, 1 - my_core)
                arrived(block)
                use(block)
        yield
        for copy in started:
            copy.wait_send()

    totals = [jnp.zeros((rows, 1), f32), jnp.zeros((rows, LANES), f32)]

    def use_hidden(block):
        values = hid_all[block]
        wide = values.astype(f32)
        totals[0] += jnp.sum(wide * wide, axis=1, keepdims=True)
        columns = pl.ds(pl.multiple_of(block * wd, wd), wd)
        totals[1] += dot_t(values, down_split[:, columns])

    hidden_gather = gather(hid_all, hid_send, hid_recv, use_hidden)
    next(hidden_gather)

    loads[2].wait()
    for p in range(n):
        oup_out[p] = oup[:, p * wd : (p + 1) * wd].astype(bf16)
    mine = pl.ds(pl.multiple_of(me * RANK, RANK), RANK)
    oup_in[mine, :] = oup_out[me]

    def oup_copy(k):
        peer = lax.rem(me + k, n)
        return push(oup_out.at[peer], oup_in.at[mine, :], oup_send.at[k], oup_recv.at[me], peer)

    def start_oup(k, carry):
        oup_copy(k).start()
        return carry

    lax.fori_loop(1, n, start_oup, 0)

    lora_rows = 3 * RANK
    down_split[2 * lora_rows :, :] = jnp.zeros((LANES - 2 * lora_rows, width), bf16)
    odown_split[2 * RANK :, :] = jnp.zeros((LANES - 2 * RANK, width), bf16)
    loads[0].wait()
    for start in range(0, width, 1024):
        columns = pl.ds(start, 1024)
        high, low = split(down[:, columns] * gain_ref[:, columns])
        down_split[:lora_rows, columns] = high
        down_split[lora_rows : 2 * lora_rows, columns] = low

    next(hidden_gather)

    inverse = lax.rsqrt(totals[0] * (1.0 / width) + epsilon)
    shrink = (totals[1] + pltpu.roll(totals[1], LANES - lora_rows, 1)) * inverse
    shrink_q = split((shrink * own_keep_ordered)[:, :RANK])
    shrink_k = split((pltpu.roll(shrink, LANES - RANK, 1) * own_keep_ordered)[:, :RANK])
    shrink_v = split((pltpu.roll(shrink, LANES - 2 * RANK, 1) * own_keep_ordered)[:, :RANK])
    gain_mine = gain_ref[:, pl.ds(pl.multiple_of(me * wd, wd), wd)]
    normed_ref[...] = (hid_all[me].astype(f32) * gain_mine * inverse).astype(bf16)
    loads[3].wait()
    loads[4].wait()

    def widen(shrunk, factors):
        high, low = split(factors)
        return dot(shrunk[0], high) + dot(shrunk[1], high) + dot(shrunk[0], low)

    rows_core, rows_y = rows // 2, rows // 4
    half_chunk = CHUNK // 2

    def core_copy(c):
        return push(core_out.at[c], core_in.at[c], core_send.at[c], core_recv.at[c], core_peer)

    def y_copy(c):
        return push(y_out.at[c], y_in.at[c], y_send.at[c], y_recv.at[c], y_peer)

    def z_copy(c, k):
        z = lax.rem(my_z + k, depth)
        return push(
            z_out.at[c, z],
            z_in.at[c, my_z],
            z_send.at[c, k],
            z_recv.at[c, my_z],
            at(z, my_y, my_core),
        )

    def project(c):
        load_w[c].wait()
        if c < QUERY_CHUNKS:
            lora = [(shrink_q, qup[:, c * CHUNK : (c + 1) * CHUNK], 0, CHUNK)]
        else:
            lora = [(shrink_k, kvup[0], 0, half_chunk), (shrink_v, kvup[1], half_chunk, half_chunk)]
        for shrunk, factors, first, size in lora:
            part[c, :, first : first + size] = dot(
                normed_ref[...], wqkv[c, :, first : first + size]
            ) + widen(shrunk, factors)
        other = pl.ds(pl.multiple_of((1 - my_core) * rows_core, rows_core), rows_core)
        core_out[c] = part[c, other, :].astype(bf16)
        core_copy(c).start()

    def add_core(c):
        core_copy(c).wait_recv()
        own = pl.ds(pl.multiple_of(my_core * rows_core, rows_core), rows_core)
        half[c] = part[c, own, :] + core_in[c].astype(f32)
        other = half[c, pl.ds(pl.multiple_of((1 - my_y) * rows_y, rows_y), rows_y), :]
        y_out[c] = jnp.concatenate([other[:, :half_chunk], other[:, half_chunk:]], axis=0).astype(bf16)
        y_copy(c).start()

    def add_y(c):
        y_copy(c).wait_recv()
        own = half[c, pl.ds(pl.multiple_of(my_y * rows_y, rows_y), rows_y), :]
        arrived = y_in[c].astype(f32)
        quarter[c, :, :half_chunk] = own[:, :half_chunk] + arrived[:rows_y]
        quarter[c, :, half_chunk:] = own[:, half_chunk:] + arrived[rows_y:]
        for z in range(depth):
            for j in range(CHUNK_HEADS):
                z_rows[c, z, STEPS * j : STEPS * (j + 1), :] = quarter[
                    c, STEPS * z : STEPS * (z + 1), HEAD_DIM * j : HEAD_DIM * (j + 1)
                ]
        z_out[c] = z_rows[c].astype(bf16)
        for k in range(1, depth):
            z_copy(c, k).start()

    def add_z(c):
        total = z_rows[c, my_z]
        for k in range(1, depth):
            z = lax.rem(my_z + k, depth)
            push(
                z_out.at[c, z], z_in.at[c, z], z_send.at[c, k], z_recv.at[c, z], core_peer
            ).wait_recv()
            total += z_in[c, z].astype(f32)
        return total.astype(bf16)

    for step in range(CHUNKS + 4):
        if step < CHUNKS:
            project(order[step])
        if 0 <= step - 2 < CHUNKS:
            add_core(order[step - 2])
        if 0 <= step - 4 < CHUNKS:
            add_y(order[step - 4])

    loads[1].wait()
    for start in range(0, width, 1024):
        columns = pl.ds(start, 1024)
        high, low = split(odown[:, columns])
        odown_split[:RANK, columns] = high
        odown_split[RANK : 2 * RANK, columns] = low

    load_cache.wait()
    kv_rows[...] = add_z(QUERY_CHUNKS).astype(f32)
    group_rows = GROUP * STEPS
    positions = cache.shape[0]
    scale = HEAD_DIM ** (-0.5)
    valid = lax.broadcasted_iota(jnp.int32, (group_rows, positions), 1) < length_ref[...]
    first_step = (lax.broadcasted_iota(jnp.int32, (group_rows, 1), 0) & (STEPS - 1)) == 0
    kv_width = KV_HEADS * HEAD_DIM
    for c in range(QUERY_CHUNKS):
        queries_all = add_z(c)
        for g in range(CHUNK_HEADS // GROUP):
            head = c * (CHUNK_HEADS // GROUP) + g
            queries = queries_all[g * group_rows : (g + 1) * group_rows]
            columns = slice(head * HEAD_DIM, (head + 1) * HEAD_DIM)
            value_columns = slice(kv_width + head * HEAD_DIM, kv_width + (head + 1) * HEAD_DIM)
            keys = [kv_rows[STEPS * head + t : STEPS * head + t + 1, :] for t in range(STEPS)]
            fresh_at = STEPS * (KV_HEADS + head)
            values = [kv_rows[fresh_at + t : fresh_at + t + 1, :] for t in range(STEPS)]
            scores = jnp.where(valid, dot_t(queries, cache[:, columns]) * scale, -1e30)
            wide = queries.astype(f32)
            fresh = [jnp.sum(wide * key, axis=1, keepdims=True) * scale for key in keys]
            fresh[1] = jnp.where(first_step, -1e30, fresh[1])
            top = jnp.maximum(jnp.max(scores, axis=1, keepdims=True), jnp.maximum(*fresh))
            exps = jnp.exp(scores - top)
            fresh = [jnp.exp(s - top) for s in fresh]
            total = jnp.sum(exps, axis=1, keepdims=True) + fresh[0] + fresh[1]
            result = dot((exps / total).astype(bf16), cache[:, value_columns])
            for s, value in zip(fresh, values):
                result += (s / total).astype(bf16).astype(f32) * value
            att_all[me, pl.ds(head * group_rows, group_rows), :] = result.astype(bf16)

    att_block = HEADS * STEPS

    def use_attended(block):
        att_rows[pl.ds(pl.multiple_of(block * att_block, att_block), att_block), :] = att_all[
            block
        ].astype(f32)

    attended_gather = gather(att_all, att_send, att_recv, use_attended)
    next(attended_gather)
    for t in range(STEPS):
        for j in range(CHUNK_HEADS):
            kv_flat[t : t + 1, HEAD_DIM * j : HEAD_DIM * (j + 1)] = kv_rows[
                STEPS * j + t : STEPS * j + t + 1, :
            ]
    newkv_ref[...] = kv_flat[...].astype(bf16)
    next(attended_gather)

    for h in range(HEADS):
        for t in range(STEPS):
            att[t * n : (t + 1) * n, h * HEAD_DIM : (h + 1) * HEAD_DIM] = att_rows[
                pl.ds(STEPS * h + t, n, stride=att_block), :
            ].astype(bf16)

    shrunk = dot_t(att[...], odown_split[...])
    shrunk = (shrunk + pltpu.roll(shrunk, LANES - RANK, 1)) * own_keep
    spots = LANES // RANK
    packed = []
    for q in range(max(1, rows // (8 * spots))):
        groups = min(spots, rows // 8 - q * spots)
        total = jnp.zeros((8, LANES), f32)
        for g in range(groups):
            first = 8 * (q * spots + g)
            piece = shrunk[first : first + 8]
            total += piece if g == 0 else pltpu.roll(piece, RANK * g, 1)
        packed.append(total)
    small[me] = packed[0] if len(packed) == 1 else jnp.concatenate(packed, axis=0)

    def small_copy(k):
        peer = lax.rem(me + k, n)
        return push(small.at[me], small.at[me], small_send.at[k], small_recv.at[me], peer)

    def start_small(k, carry):
        small_copy(k).start()
        return carry

    lax.fori_loop(1, n, start_small, 0)

    load_wout.wait()
    base = dot(att[...], wout[...]) + hid_ref[...].astype(f32)

    def end_oup(k, carry):
        other = lax.rem(me + k, n)
        theirs = pl.ds(pl.multiple_of(other * RANK, RANK), RANK)
        push(
            oup_out.at[other], oup_in.at[theirs, :], oup_send.at[k], oup_recv.at[other], other
        ).wait()
        return carry

    lax.fori_loop(1, n, end_oup, 0)

    def end_small(k, carry):
        other = lax.rem(me + k, n)
        push(small.at[other], small.at[other], small_send.at[k], small_recv.at[other], other).wait()
        return carry

    lax.fori_loop(1, n, end_small, 0)

    whole = small[0]
    for p in range(1, n):
        whole += small[p]
    pieces = []
    for i in range(rows // 8):
        q, g = divmod(i, spots)
        piece = whole[8 * q : 8 * q + 8]
        pieces.append(piece if g == 0 else pltpu.roll(piece, LANES - RANK * g, 1))
    rows_out = jnp.where(lane < RANK, jnp.concatenate(pieces, axis=0), 0.0)
    reach = RANK
    while reach < LANES:
        rows_out += pltpu.roll(rows_out, reach, 1)
        reach *= 2
    spread = jnp.concatenate([rows_out] * (n * RANK // LANES), axis=1)
    place_of = lax.broadcasted_iota(jnp.int32, (rows, n * RANK), 1) >> (RANK.bit_length() - 1)
    high, low = split(jnp.where(place_of.astype(f32) == slot_of, spread, 0.0))
    update = dot(high, oup_in[...]) + dot(low, oup_in[...])
    out_ref[...] = (base + update).astype(bf16)

    for gathered in (hidden_gather, attended_gather):
        for _ in gathered:
            pass
    for c in range(CHUNKS):
        core_copy(c).wait_send()
        y_copy(c).wait_send()
        for k in range(1, depth):
            z_copy(c, k).wait_send()


def hand_over(rows_ref, kv_ref, rows_out, kv_out):
    rows_out[...] = rows_ref[...]
    kv_out[...] = kv_ref[...]


def local(
    n,
    hidden,
    norm_gain_vector,
    query_key_value_weight,
    output_weight,
    key_value_cache,
    cache_valid_length,
    request_adapter_index,
    adapter_slot_place,
    adapter_rank_used,
    adapter_down_factor,
    query_up_factor,
    key_value_up_factor,
    output_down_factor,
    output_up_factor,
):
    steps, requests, wd = hidden.shape
    width = norm_gain_vector.shape[0]
    positions = key_value_cache.shape[1]
    assert steps == STEPS and requests == n and adapter_down_factor.shape[0] == 1 and wd * n == width
    rows, depth = steps * n, n // 4
    att_block = HEADS * STEPS
    sends = 4 * depth
    packed_rows = 8 * max(1, rows * RANK // (8 * LANES))
    vmem = pl.BlockSpec(memory_space=pltpu.VMEM)
    hbm = pl.BlockSpec(memory_space=pl.ANY)
    dma = pltpu.SemaphoreType.DMA
    out, new_kv = pl.pallas_call(
        functools.partial(kernel, n, width),
        out_shape=(
            jax.ShapeDtypeStruct((rows, wd), bf16),
            jax.ShapeDtypeStruct((STEPS, CHUNK), bf16),
        ),
        in_specs=[vmem] * 6 + [hbm] * 8,
        out_specs=(vmem, vmem),
        scratch_shapes=[
            pltpu.VMEM((CHUNKS, wd, CHUNK), bf16),
            pltpu.VMEM((width, wd), bf16),
            pltpu.VMEM((positions, CHUNK), bf16),
            pltpu.VMEM((3 * RANK, width), f32),
            pltpu.VMEM((RANK, width), f32),
            pltpu.VMEM((2, RANK, CHUNK // 2), f32),
            pltpu.VMEM((RANK, width), f32),
            pltpu.VMEM((RANK, width), f32),
            pltpu.VMEM((LANES, width), bf16),
            pltpu.VMEM((LANES, width), bf16),
            pltpu.VMEM((n, rows, wd), bf16),
            pltpu.VMEM((rows, wd), bf16),
            pltpu.VMEM((CHUNKS, rows, CHUNK), f32),
            pltpu.VMEM((CHUNKS, rows // 2, CHUNK), bf16),
            pltpu.VMEM((CHUNKS, rows // 2, CHUNK), bf16),
            pltpu.VMEM((CHUNKS, rows // 2, CHUNK), f32),
            pltpu.VMEM((CHUNKS, rows // 2, CHUNK // 2), bf16),
            pltpu.VMEM((CHUNKS, rows // 2, CHUNK // 2), bf16),
            pltpu.VMEM((CHUNKS, rows // 4, CHUNK), f32),
            pltpu.VMEM((CHUNKS, depth, PACKED, HEAD_DIM), f32),
            pltpu.VMEM((CHUNKS, depth, PACKED, HEAD_DIM), bf16),
            pltpu.VMEM((CHUNKS, depth, PACKED, HEAD_DIM), bf16),
            pltpu.VMEM((PACKED, HEAD_DIM), f32),
            pltpu.VMEM((STEPS, CHUNK), f32),
            pltpu.VMEM((n, att_block, HEAD_DIM), bf16),
            pltpu.VMEM((n * att_block, HEAD_DIM), f32),
            pltpu.VMEM((rows, HEADS * HEAD_DIM), bf16),
            pltpu.VMEM((n, RANK, wd), bf16),
            pltpu.VMEM((n * RANK, wd), bf16),
            pltpu.VMEM((n, packed_rows, LANES), f32),
            dma((5 + CHUNKS + 2,)),
            dma((sends,)),
            dma((n,)),
            dma((sends,)),
            dma((n,)),
            dma((CHUNKS,)),
            dma((CHUNKS,)),
            dma((CHUNKS,)),
            dma((CHUNKS,)),
            dma((CHUNKS, depth)),
            dma((CHUNKS, depth)),
            dma((n,)),
            dma((n,)),
            dma((n,)),
            dma((n,)),
        ],
        compiler_params=pltpu.CompilerParams(
            collective_id=0, has_side_effects=True, vmem_limit_bytes=56 * 1024 * 1024
        ),
        cost_estimate=pl.CostEstimate(
            flops=2 * rows * 18 * 1024 * width // n * 8, bytes_accessed=24 << 20, transcendentals=0
        ),
    )(
        hidden.reshape(rows, wd),
        norm_gain_vector.reshape(1, width),
        cache_valid_length.reshape(1, 1),
        request_adapter_index.transpose(0, 2, 1),
        adapter_slot_place.reshape(1, -1),
        adapter_rank_used.reshape(1, -1),
        query_key_value_weight,
        output_weight,
        key_value_cache.reshape(positions, CHUNK),
        adapter_down_factor.reshape(3 * RANK, width),
        query_up_factor.reshape(RANK, width),
        key_value_up_factor.reshape(2, RANK, CHUNK // 2),
        output_down_factor.reshape(RANK, width),
        output_up_factor.reshape(RANK, width),
    )
    out, new_kv = pl.pallas_call(
        hand_over,
        out_shape=(
            jax.ShapeDtypeStruct((rows, wd), bf16),
            jax.ShapeDtypeStruct((STEPS, CHUNK), bf16),
        ),
        in_specs=[vmem, vmem],
        out_specs=(vmem, vmem),
    )(out, new_kv)
    return out.reshape(steps, requests, wd), new_kv.reshape(steps, 1, CHUNK)


def solution(mesh):
    placed = (
        P(None, "groups", "pool"),
        P(),
        P("pool", None),
        P(None, "pool"),
        P(("groups", "pool"), None, None),
        P(("groups", "pool")),
        P(None, "groups", None),
        P("groups"),
        P("groups"),
        P(("groups", "pool"), None, None),
        P(("groups", "pool"), None, None),
        P(("groups", "pool"), None, None, None),
        P(("groups", "pool"), None, None),
        P(("groups", "pool"), None, None),
    )
    return jax.shard_map(
        functools.partial(local, mesh.shape["pool"]),
        mesh=mesh,
        in_specs=placed,
        out_specs=(P(None, "groups", "pool"), P(None, ("groups", "pool"), None)),
        check_vma=False,
    )
```

```python
import functools

import jax
import jax.numpy as jnp
from jax import lax
from jax.experimental import pallas as pl
from jax.experimental.pallas import tpu as pltpu
from jax.sharding import PartitionSpec as P

HEADS = 64
KV_HEADS = 8
HEAD_DIM = 128
GROUP = HEADS // KV_HEADS
STEPS = 2
RANK = 16
LANES = 128
CHUNK = 2 * KV_HEADS * HEAD_DIM
QUERY_CHUNKS = HEADS * HEAD_DIM // CHUNK
CHUNKS = QUERY_CHUNKS + 1
CHUNK_HEADS = CHUNK // HEAD_DIM
PACKED = CHUNK_HEADS * STEPS

epsilon = 1e-05
f32, bf16 = jnp.float32, jnp.bfloat16


def dot(a, b):
    return jnp.dot(a, b, preferred_element_type=f32)


def dot_t(a, b):
    return lax.dot_general(a, b, (((1,), (1,)), ((), ())), preferred_element_type=f32)


def split(a):
    high = a.astype(bf16)
    return high, (a - high.astype(f32)).astype(bf16)


def kernel(
    n,
    width,
    hid_ref,
    gain_ref,
    length_ref,
    index_ref,
    place_ref,
    rank_ref,
    wqkv_hbm,
    wout_hbm,
    cache_hbm,
    down_hbm,
    qup_hbm,
    kvup_hbm,
    odown_hbm,
    oup_hbm,
    out_ref,
    newkv_ref,
    wqkv,
    wout,
    cache,
    down,
    qup,
    kvup,
    odown,
    oup,
    down_split,
    odown_split,
    hid_all,
    normed_ref,
    part,
    core_out,
    core_in,
    half,
    y_out,
    y_in,
    quarter,
    z_rows,
    z_out,
    z_in,
    kv_rows,
    kv_flat,
    att_all,
    att_rows,
    att,
    oup_out,
    oup_in,
    small,
    load_sem,
    hid_send,
    hid_recv,
    att_send,
    att_recv,
    core_send,
    core_recv,
    y_send,
    y_recv,
    z_send,
    z_recv,
    oup_send,
    oup_recv,
    small_send,
    small_recv,
):
    me = lax.axis_index("pool")
    depth = n // 4
    my_z, my_y, my_core = me // 4, lax.rem(me // 2, 2), lax.rem(me, 2)
    rows = STEPS * n
    wd = width // n

    def at(z, y, core):
        return z * 4 + y * 2 + core

    def paired(k):
        z = my_z
        for bit in range(depth.bit_length() - 1):
            if k >> bit & 1:
                z = z + (1 << bit) * (1 - 2 * lax.rem(z // (1 << bit), 2))
        return z

    core_peer = at(my_z, my_y, 1 - my_core)
    y_peer = at(my_z, 1 - my_y, my_core)

    def push(src, dst, send, recv, peer):
        return pltpu.make_async_remote_copy(
            src_ref=src,
            dst_ref=dst,
            send_sem=send,
            recv_sem=recv,
            device_id={"pool": peer},
            device_id_type=pl.DeviceIdType.MESH,
        )

    order = [QUERY_CHUNKS] + list(range(QUERY_CHUNKS))
    loads = [
        (down_hbm, down),
        (odown_hbm, odown),
        (oup_hbm, oup),
        (qup_hbm, qup),
        (kvup_hbm, kvup),
    ]
    loads += [(wqkv_hbm.at[:, pl.ds(c * CHUNK, CHUNK)], wqkv.at[c]) for c in order]
    loads += [(cache_hbm, cache), (wout_hbm, wout)]
    loads = [pltpu.make_async_copy(s, d, load_sem.at[i]) for i, (s, d) in enumerate(loads)]
    for load in loads:
        load.start()
    load_w = dict(zip(order, loads[5:]))
    load_cache, load_wout = loads[-2:]

    barrier = pltpu.get_barrier_semaphore()

    def greet(k, carry):
        pl.semaphore_signal(
            barrier,
            inc=1,
            device_id={"pool": lax.rem(me + k, n)},
            device_id_type=pl.DeviceIdType.MESH,
        )
        return carry

    lax.fori_loop(1, n, greet, 0)

    row = lax.broadcasted_iota(jnp.int32, (rows, rows), 0)
    column = lax.broadcasted_iota(jnp.int32, (rows, rows), 1)
    z_bits = depth.bit_length() - 1
    source = (
        ((row >> z_bits) & (STEPS - 1)) * n
        + (row & (depth - 1)) * 4
        + ((row >> (1 + z_bits)) & 1) * 2
        + (row >> (2 + z_bits))
    )
    order_rows = (source == column).astype(f32)
    hid_all[me] = dot(order_rows.astype(bf16), hid_ref[...]).astype(bf16)

    lane = lax.broadcasted_iota(jnp.int32, (rows, LANES), 1)
    adapters = place_ref.shape[1]
    same = lax.broadcasted_iota(jnp.int32, (n, n), 0) == lax.broadcasted_iota(jnp.int32, (n, n), 1)
    adapter_of = jnp.concatenate(
        [
            jnp.sum(jnp.where(same, index_ref[t].astype(f32), 0.0), axis=1, keepdims=True)
            for t in range(STEPS)
        ],
        axis=0,
    )
    adapter = lax.broadcasted_iota(jnp.int32, (rows, adapters), 1)
    matches = adapter_of == adapter.astype(f32)
    slot_of = jnp.sum(jnp.where(matches, place_ref[...].astype(f32), 0.0), axis=1, keepdims=True)
    rank_of = jnp.sum(jnp.where(matches, rank_ref[...].astype(f32), 0.0), axis=1, keepdims=True)
    keep = jnp.where(lane.astype(f32) < rank_of, 4.0 / jnp.sqrt(rank_of), 0.0)
    own_keep = jnp.where(slot_of == me.astype(f32), keep, 0.0)
    own_keep_ordered = jnp.dot(
        order_rows, own_keep, precision=lax.Precision.HIGHEST, preferred_element_type=f32
    )

    lora_rows = 3 * RANK
    down_split[2 * lora_rows :, :] = jnp.zeros((LANES - 2 * lora_rows, width), bf16)
    loads[0].wait()
    for start in range(0, width, 1024):
        columns = pl.ds(start, 1024)
        high, low = split(down[:, columns] * gain_ref[:, columns])
        down_split[:lora_rows, columns] = high
        down_split[lora_rows : 2 * lora_rows, columns] = low

    loads[1].wait()
    for start in range(0, width, 1024):
        high, low = split(odown[:, pl.ds(start, 1024)])
        stacked = jnp.concatenate(
            [high.astype(f32), low.astype(f32), jnp.zeros((LANES - 2 * RANK, 1024), f32)], axis=0
        )
        odown_split[pl.ds(start, 1024), :] = stacked.T.astype(bf16)

    loads[2].wait()
    for p in range(n):
        oup_out[p] = oup[:, p * wd : (p + 1) * wd].astype(bf16)
    mine = pl.ds(pl.multiple_of(me * RANK, RANK), RANK)
    oup_in[mine, :] = oup_out[me]

    def oup_copy(k):
        peer = lax.rem(me + k, n)
        return push(oup_out.at[peer], oup_in.at[mine, :], oup_send.at[k], oup_recv.at[me], peer)

    pl.semaphore_wait(barrier, n - 1)

    def gather(buffer, send, recv, use):
        started = []

        def start(block, peer):
            copy = push(buffer.at[block], buffer.at[block], send.at[len(started)], recv.at[block], peer)
            copy.start()
            started.append(copy)

        def arrived(block):
            push(buffer.at[block], buffer.at[block], send.at[0], recv.at[block], core_peer).wait_recv()

        for k in range(depth - 1, 0, -1):
            start(me, at(paired(k), my_y, my_core))
        start(me, y_peer)
        start(me, core_peer)
        yield
        use(me)
        for k in range(1, depth):
            block = at(paired(k), my_y, my_core)
            arrived(block)
            start(block, y_peer)
            start(block, core_peer)
            use(block)
        for k in range(depth):
            block = at(paired(k), 1 - my_y, my_core)
            arrived(block)
            start(block, core_peer)
            use(block)
        for y in (my_y, 1 - my_y):
            for k in range(depth):
                block = at(paired(k), y, 1 - my_core)
                arrived(block)
                use(block)
        yield
        for copy in started:
            copy.wait_send()

    totals = [jnp.zeros((rows, 1), f32), jnp.zeros((rows, LANES), f32)]

    def use_hidden(block):
        values = hid_all[block]
        wide = values.astype(f32)
        totals[0] += jnp.sum(wide * wide, axis=1, keepdims=True)
        columns = pl.ds(pl.multiple_of(block * wd, wd), wd)
        totals[1] += dot_t(values, down_split[:, columns])

    hidden_gather = gather(hid_all, hid_send, hid_recv, use_hidden)
    next(hidden_gather)
    def start_oup(k, carry):
        oup_copy(k).start()
        return carry

    lax.fori_loop(1, n, start_oup, 0)


    next(hidden_gather)

    inverse = lax.rsqrt(totals[0] * (1.0 / width) + epsilon)
    shrink = (totals[1] + pltpu.roll(totals[1], LANES - lora_rows, 1)) * inverse
    shrink_q = split((shrink * own_keep_ordered)[:, :RANK])
    shrink_k = split((pltpu.roll(shrink, LANES - RANK, 1) * own_keep_ordered)[:, :RANK])
    shrink_v = split((pltpu.roll(shrink, LANES - 2 * RANK, 1) * own_keep_ordered)[:, :RANK])
    gain_mine = gain_ref[:, pl.ds(pl.multiple_of(me * wd, wd), wd)]
    normed_ref[...] = (hid_all[me].astype(f32) * gain_mine * inverse).astype(bf16)
    loads[3].wait()
    loads[4].wait()

    def widen(shrunk, factors):
        high, low = split(factors)
        return dot(shrunk[0], high) + dot(shrunk[1], high) + dot(shrunk[0], low)

    rows_core, rows_y = rows // 2, rows // 4
    half_chunk = CHUNK // 2

    def core_copy(c):
        return push(core_out.at[c], core_in.at[c], core_send.at[c], core_recv.at[c], core_peer)

    def y_copy(c):
        return push(y_out.at[c], y_in.at[c], y_send.at[c], y_recv.at[c], y_peer)

    def z_copy(c, k):
        z = paired(k)
        return push(
            z_out.at[c, z],
            z_in.at[c, my_z],
            z_send.at[c, k],
            z_recv.at[c, my_z],
            at(z, my_y, my_core),
        )

    def project(c):
        load_w[c].wait()
        if c < QUERY_CHUNKS:
            lora = [(shrink_q, qup[:, c * CHUNK : (c + 1) * CHUNK], 0, CHUNK)]
        else:
            lora = [(shrink_k, kvup[0], 0, half_chunk), (shrink_v, kvup[1], half_chunk, half_chunk)]
        for shrunk, factors, first, size in lora:
            part[c, :, first : first + size] = dot(
                normed_ref[...], wqkv[c, :, first : first + size]
            ) + widen(shrunk, factors)
        other = pl.ds(pl.multiple_of((1 - my_core) * rows_core, rows_core), rows_core)
        core_out[c] = part[c, other, :].astype(bf16)
        core_copy(c).start()

    def add_core(c):
        core_copy(c).wait_recv()
        own = pl.ds(pl.multiple_of(my_core * rows_core, rows_core), rows_core)
        half[c] = part[c, own, :] + core_in[c].astype(f32)
        other = half[c, pl.ds(pl.multiple_of((1 - my_y) * rows_y, rows_y), rows_y), :]
        y_out[c] = jnp.concatenate([other[:, :half_chunk], other[:, half_chunk:]], axis=0).astype(bf16)
        y_copy(c).start()

    def add_y(c):
        y_copy(c).wait_recv()
        own = half[c, pl.ds(pl.multiple_of(my_y * rows_y, rows_y), rows_y), :]
        arrived = y_in[c].astype(f32)
        quarter[c, :, :half_chunk] = own[:, :half_chunk] + arrived[:rows_y]
        quarter[c, :, half_chunk:] = own[:, half_chunk:] + arrived[rows_y:]
        for t in range(STEPS):
            for j in range(CHUNK_HEADS):
                z_rows[c, pl.ds(STEPS * j + t, depth, stride=PACKED), :] = quarter[
                    c, depth * t : depth * (t + 1), HEAD_DIM * j : HEAD_DIM * (j + 1)
                ]
        z_out[c] = z_rows[c].reshape(depth, PACKED, HEAD_DIM).astype(bf16)
        for k in range(depth - 1, 0, -1):
            z_copy(c, k).start()

    def add_z(c):
        total = z_rows[c, pl.ds(pl.multiple_of(my_z * PACKED, PACKED), PACKED), :]
        for k in range(1, depth):
            z = paired(k)
            push(
                z_out.at[c, z], z_in.at[c, z], z_send.at[c, k], z_recv.at[c, z], core_peer
            ).wait_recv()
            total += z_in[c, z].astype(f32)
        return total.astype(bf16)

    for step in range(CHUNKS + 4):
        if step < CHUNKS:
            project(order[step])
        if 0 <= step - 2 < CHUNKS:
            add_core(order[step - 2])
        if 0 <= step - 4 < CHUNKS:
            add_y(order[step - 4])

    load_cache.wait()
    kv_rows[...] = add_z(QUERY_CHUNKS).astype(f32)
    group_rows = GROUP * STEPS
    positions = cache.shape[0]
    scale = HEAD_DIM ** (-0.5)
    valid = lax.broadcasted_iota(jnp.int32, (group_rows, positions), 1) < length_ref[...]
    first_step = (lax.broadcasted_iota(jnp.int32, (group_rows, 1), 0) & (STEPS - 1)) == 0
    kv_width = KV_HEADS * HEAD_DIM
    for c in range(QUERY_CHUNKS):
        queries_all = add_z(c)
        for g in range(CHUNK_HEADS // GROUP):
            head = c * (CHUNK_HEADS // GROUP) + g
            queries = queries_all[g * group_rows : (g + 1) * group_rows]
            columns = slice(head * HEAD_DIM, (head + 1) * HEAD_DIM)
            value_columns = slice(kv_width + head * HEAD_DIM, kv_width + (head + 1) * HEAD_DIM)
            keys = [kv_rows[STEPS * head + t : STEPS * head + t + 1, :] for t in range(STEPS)]
            fresh_at = STEPS * (KV_HEADS + head)
            values = [kv_rows[fresh_at + t : fresh_at + t + 1, :] for t in range(STEPS)]
            scores = jnp.where(valid, dot_t(queries, cache[:, columns]) * scale, -1e30)
            wide = queries.astype(f32)
            fresh = [jnp.sum(wide * key, axis=1, keepdims=True) * scale for key in keys]
            fresh[1] = jnp.where(first_step, -1e30, fresh[1])
            top = jnp.maximum(jnp.max(scores, axis=1, keepdims=True), jnp.maximum(*fresh))
            exps = jnp.exp(scores - top)
            fresh = [jnp.exp(s - top) for s in fresh]
            total = jnp.sum(exps, axis=1, keepdims=True) + fresh[0] + fresh[1]
            result = dot((exps / total).astype(bf16), cache[:, value_columns])
            for s, value in zip(fresh, values):
                result += (s / total).astype(bf16).astype(f32) * value
            att_all[me, pl.ds(head * group_rows, group_rows), :] = result.astype(bf16)

    att_block = HEADS * STEPS

    def use_attended(block):
        att_rows[pl.ds(pl.multiple_of(block * att_block, att_block), att_block), :] = att_all[
            block
        ].astype(f32)

    attended_gather = gather(att_all, att_send, att_recv, use_attended)
    next(attended_gather)
    for t in range(STEPS):
        for j in range(CHUNK_HEADS):
            kv_flat[t : t + 1, HEAD_DIM * j : HEAD_DIM * (j + 1)] = kv_rows[
                STEPS * j + t : STEPS * j + t + 1, :
            ]
    newkv_ref[...] = kv_flat[...].astype(bf16)
    next(attended_gather)

    for h in range(HEADS):
        for t in range(STEPS):
            att[t * n : (t + 1) * n, h * HEAD_DIM : (h + 1) * HEAD_DIM] = att_rows[
                pl.ds(STEPS * h + t, n, stride=att_block), :
            ].astype(bf16)

    shrunk = dot(att[...], odown_split[...])
    shrunk = (shrunk + pltpu.roll(shrunk, LANES - RANK, 1)) * own_keep
    spots = LANES // RANK
    packed = []
    for q in range(max(1, rows // (8 * spots))):
        groups = min(spots, rows // 8 - q * spots)
        total = jnp.zeros((8, LANES), f32)
        for g in range(groups):
            first = 8 * (q * spots + g)
            piece = shrunk[first : first + 8]
            total += piece if g == 0 else pltpu.roll(piece, RANK * g, 1)
        packed.append(total)
    small[me] = packed[0] if len(packed) == 1 else jnp.concatenate(packed, axis=0)

    def small_copy(k):
        peer = lax.rem(me + k, n)
        return push(small.at[me], small.at[me], small_send.at[k], small_recv.at[me], peer)

    def start_small(k, carry):
        small_copy(k).start()
        return carry

    lax.fori_loop(1, n, start_small, 0)

    load_wout.wait()
    base = dot(att[...], wout[...]) + hid_ref[...].astype(f32)

    def end_oup(k, carry):
        other = lax.rem(me + k, n)
        theirs = pl.ds(pl.multiple_of(other * RANK, RANK), RANK)
        push(
            oup_out.at[other], oup_in.at[theirs, :], oup_send.at[k], oup_recv.at[other], other
        ).wait()
        return carry

    lax.fori_loop(1, n, end_oup, 0)

    def end_small(k, carry):
        other = lax.rem(me + k, n)
        push(small.at[other], small.at[other], small_send.at[k], small_recv.at[other], other).wait()
        return carry

    lax.fori_loop(1, n, end_small, 0)

    whole = small[0]
    for p in range(1, n):
        whole += small[p]
    pieces = []
    for i in range(rows // 8):
        q, g = divmod(i, spots)
        piece = whole[8 * q : 8 * q + 8]
        pieces.append(piece if g == 0 else pltpu.roll(piece, LANES - RANK * g, 1))
    rows_out = jnp.where(lane < RANK, jnp.concatenate(pieces, axis=0), 0.0)
    reach = RANK
    while reach < LANES:
        rows_out += pltpu.roll(rows_out, reach, 1)
        reach *= 2
    spread = jnp.concatenate([rows_out] * (n * RANK // LANES), axis=1)
    place_of = lax.broadcasted_iota(jnp.int32, (rows, n * RANK), 1) >> (RANK.bit_length() - 1)
    high, low = split(jnp.where(place_of.astype(f32) == slot_of, spread, 0.0))
    update = dot(high, oup_in[...]) + dot(low, oup_in[...])
    out_ref[...] = (base + update).astype(bf16)

    for gathered in (hidden_gather, attended_gather):
        for _ in gathered:
            pass
    for c in range(CHUNKS):
        core_copy(c).wait_send()
        y_copy(c).wait_send()
        for k in range(1, depth):
            z_copy(c, k).wait_send()


def hand_over(rows_ref, kv_ref, rows_out, kv_out):
    rows_out[...] = rows_ref[...]
    kv_out[...] = kv_ref[...]


def local(
    n,
    hidden,
    norm_gain_vector,
    query_key_value_weight,
    output_weight,
    key_value_cache,
    cache_valid_length,
    request_adapter_index,
    adapter_slot_place,
    adapter_rank_used,
    adapter_down_factor,
    query_up_factor,
    key_value_up_factor,
    output_down_factor,
    output_up_factor,
):
    steps, requests, wd = hidden.shape
    width = norm_gain_vector.shape[0]
    positions = key_value_cache.shape[1]
    assert steps == STEPS and requests == n and adapter_down_factor.shape[0] == 1 and wd * n == width
    rows, depth = steps * n, n // 4
    att_block = HEADS * STEPS
    sends = 4 * depth
    packed_rows = 8 * max(1, rows * RANK // (8 * LANES))
    vmem = pl.BlockSpec(memory_space=pltpu.VMEM)
    hbm = pl.BlockSpec(memory_space=pl.ANY)
    dma = pltpu.SemaphoreType.DMA
    out, new_kv = pl.pallas_call(
        functools.partial(kernel, n, width),
        out_shape=(
            jax.ShapeDtypeStruct((rows, wd), bf16),
            jax.ShapeDtypeStruct((STEPS, CHUNK), bf16),
        ),
        in_specs=[vmem] * 6 + [hbm] * 8,
        out_specs=(vmem, vmem),
        scratch_shapes=[
            pltpu.VMEM((CHUNKS, wd, CHUNK), bf16),
            pltpu.VMEM((width, wd), bf16),
            pltpu.VMEM((positions, CHUNK), bf16),
            pltpu.VMEM((3 * RANK, width), f32),
            pltpu.VMEM((RANK, width), f32),
            pltpu.VMEM((2, RANK, CHUNK // 2), f32),
            pltpu.VMEM((RANK, width), f32),
            pltpu.VMEM((RANK, width), f32),
            pltpu.VMEM((LANES, width), bf16),
            pltpu.VMEM((width, LANES), bf16),
            pltpu.VMEM((n, rows, wd), bf16),
            pltpu.VMEM((rows, wd), bf16),
            pltpu.VMEM((CHUNKS, rows, CHUNK), f32),
            pltpu.VMEM((CHUNKS, rows // 2, CHUNK), bf16),
            pltpu.VMEM((CHUNKS, rows // 2, CHUNK), bf16),
            pltpu.VMEM((CHUNKS, rows // 2, CHUNK), f32),
            pltpu.VMEM((CHUNKS, rows // 2, CHUNK // 2), bf16),
            pltpu.VMEM((CHUNKS, rows // 2, CHUNK // 2), bf16),
            pltpu.VMEM((CHUNKS, rows // 4, CHUNK), f32),
            pltpu.VMEM((CHUNKS, depth * PACKED, HEAD_DIM), f32),
            pltpu.VMEM((CHUNKS, depth, PACKED, HEAD_DIM), bf16),
            pltpu.VMEM((CHUNKS, depth, PACKED, HEAD_DIM), bf16),
            pltpu.VMEM((PACKED, HEAD_DIM), f32),
            pltpu.VMEM((STEPS, CHUNK), f32),
            pltpu.VMEM((n, att_block, HEAD_DIM), bf16),
            pltpu.VMEM((n * att_block, HEAD_DIM), f32),
            pltpu.VMEM((rows, HEADS * HEAD_DIM), bf16),
            pltpu.VMEM((n, RANK, wd), bf16),
            pltpu.VMEM((n * RANK, wd), bf16),
            pltpu.VMEM((n, packed_rows, LANES), f32),
            dma((5 + CHUNKS + 2,)),
            dma((sends,)),
            dma((n,)),
            dma((sends,)),
            dma((n,)),
            dma((CHUNKS,)),
            dma((CHUNKS,)),
            dma((CHUNKS,)),
            dma((CHUNKS,)),
            dma((CHUNKS, depth)),
            dma((CHUNKS, depth)),
            dma((n,)),
            dma((n,)),
            dma((n,)),
            dma((n,)),
        ],
        compiler_params=pltpu.CompilerParams(
            collective_id=0, has_side_effects=True, vmem_limit_bytes=56 * 1024 * 1024
        ),
        cost_estimate=pl.CostEstimate(
            flops=2 * rows * 18 * 1024 * width // n * 8, bytes_accessed=24 << 20, transcendentals=0
        ),
    )(
        hidden.reshape(rows, wd),
        norm_gain_vector.reshape(1, width),
        cache_valid_length.reshape(1, 1),
        request_adapter_index.transpose(0, 2, 1),
        adapter_slot_place.reshape(1, -1),
        adapter_rank_used.reshape(1, -1),
        query_key_value_weight,
        output_weight,
        key_value_cache.reshape(positions, CHUNK),
        adapter_down_factor.reshape(3 * RANK, width),
        query_up_factor.reshape(RANK, width),
        key_value_up_factor.reshape(2, RANK, CHUNK // 2),
        output_down_factor.reshape(RANK, width),
        output_up_factor.reshape(RANK, width),
    )
    out, new_kv = pl.pallas_call(
        hand_over,
        out_shape=(
            jax.ShapeDtypeStruct((rows, wd), bf16),
            jax.ShapeDtypeStruct((STEPS, CHUNK), bf16),
        ),
        in_specs=[vmem, vmem],
        out_specs=(vmem, vmem),
    )(out, new_kv)
    return out.reshape(steps, requests, wd), new_kv.reshape(steps, 1, CHUNK)


def solution(mesh):
    placed = (
        P(None, "groups", "pool"),
        P(),
        P("pool", None),
        P(None, "pool"),
        P(("groups", "pool"), None, None),
        P(("groups", "pool")),
        P(None, "groups", None),
        P("groups"),
        P("groups"),
        P(("groups", "pool"), None, None),
        P(("groups", "pool"), None, None),
        P(("groups", "pool"), None, None, None),
        P(("groups", "pool"), None, None),
        P(("groups", "pool"), None, None),
    )
    return jax.shard_map(
        functools.partial(local, mesh.shape["pool"]),
        mesh=mesh,
        in_specs=placed,
        out_specs=(P(None, "groups", "pool"), P(None, ("groups", "pool"), None)),
        check_vma=False,
    )
```
